32 devices in a mesh: gen: 8 (over z, x), split: 4 (over y, core).
Axes of the slice: x: 2, y: 2, z: 4, core: 2. Of those that a mesh axis runs over, the one named last changes fastest.
Arguments:
- hidden: bfloat16 [32, 256, 8192], P(None, 'gen', 'split'), may hold values from -12 to 12
- w_proj: bfloat16 [8192, 1024], P('split', 'gen'), may hold values from -0.0625 to 0.0625
- slot_prompt: int32 [256], P('gen'), may hold values from 0 to 7, as said below
- lengths: int32 [256], P('gen'), may hold values from 1 to 32
- weights: bfloat16 [256], P('gen'), may hold values from 0.099609375 to 10
- owner: int32 [8], replicated, may hold values from 0 to 7, each once
Outputs:
- utility: float32 [8, 64], P('gen')
The draws below stay inside these ranges and needn't reach their ends.
Inputs may be any that keep to these rules, and one draw needn't show every extreme that they name: `slot_prompt`: each prompt names 1 to 64 slots and one prompt names exactly 64; each generator device (a run of 32 slots) holds at most 8 slots of one prompt, and some device holds exactly 8. `owner`: each index along gen owns exactly one prompt.
All inputs are finite; a program needn't handle non-finite values.
Results may differ from the reference program's by a relative error of at most 0.0015.
Values may be sent and summed in bfloat16 or wider, within the bound.
A program may use at most 64 MiB of HBM per device.

```python
import math
import jax
import jax.numpy as jnp
from jax import lax

HID = 8192
EMB = 1024
SEQ = 32
SLOTS = 32
MAXS = 64
NS = 256
N_GEN = 8
N_SPLIT = 4


def slot_prompts(key):
    heat_key = jax.random.fold_in(key, 11)
    noise_key = jax.random.fold_in(key, 12)
    home_key = jax.random.fold_in(key, 13)
    order_key = jax.random.fold_in(key, 14)
    full_key = jax.random.fold_in(key, 15)
    prompts = N_GEN
    extra = MAXS - 1
    cells = prompts * extra
    heat = jax.random.randint(heat_key, (prompts,), 0, 4)
    full_prompt = jax.random.randint(full_key, (), 0, prompts)
    noise = jax.random.randint(noise_key, (prompts, extra), 0, 2048)
    cell_index = jnp.arange(cells, dtype=jnp.int32).reshape(prompts, extra)
    scores = (heat[:, None] * 2048 + noise) * cells + cell_index
    is_full = jnp.arange(prompts, dtype=jnp.int32) == full_prompt
    scores = jnp.where(is_full[:, None], -1, scores)
    remaining = N_GEN * SLOTS - MAXS - (prompts - 1)
    flat_scores = scores.reshape(cells)
    top_values, top_where = jax.lax.top_k(flat_scores, remaining)
    threshold = top_values[remaining - 1]
    picked = (scores >= threshold).astype(jnp.int32)
    counts = 1 + jnp.sum(picked, axis=1)
    counts = jnp.where(is_full, MAXS, counts)
    ends = jnp.cumsum(counts)
    samples = N_GEN * SLOTS
    home = jax.random.permutation(home_key, N_GEN)
    order_scores = jax.random.randint(order_key, (N_GEN, SLOTS), 0, 2 ** 20) * SLOTS + jnp.arange(SLOTS, dtype=jnp.int32)[None, :]
    arrange = jnp.argsort(order_scores, axis=1)
    residue = jnp.arange(N_GEN, dtype=jnp.int32)[:, None]
    global_index = arrange * N_GEN + residue
    prompt_of = jnp.sum((global_index.reshape(samples)[:, None] >= ends[None, :]).astype(jnp.int32), axis=1)
    target = (home[:, None] * SLOTS + jnp.arange(SLOTS, dtype=jnp.int32)[None, :]).reshape(samples)
    result = jnp.zeros((samples,), jnp.int32).at[target].set(prompt_of)
    return result


def draw_slot_prompt(key, part):
    return slot_prompts(key)


def draw_hidden(key, part):
    prompt_of = slot_prompts(key)
    samples = N_GEN * SLOTS
    direction_count = 12
    direction_pool = jax.random.normal(jax.random.fold_in(key, 21), (N_GEN * direction_count, HID), jnp.float32)
    first_direction = jax.random.randint(jax.random.fold_in(key, 22), (samples,), 0, direction_count)
    direction_span = jax.random.randint(jax.random.fold_in(key, 23), (samples,), 1, direction_count + 1)
    offsets = jax.random.randint(jax.random.fold_in(key, 24), (SEQ, samples), 0, 65536) % direction_span[None, :]
    picked_direction = (first_direction[None, :] + offsets) % direction_count
    chosen = jnp.take(direction_pool, prompt_of[None, :] * direction_count + picked_direction, axis=0)
    noise_level = jnp.exp(jax.random.uniform(jax.random.fold_in(key, 25), (samples,), jnp.float32, math.log(0.3), 0.0))
    amplitude = jax.random.uniform(jax.random.fold_in(key, 26), (SEQ, samples), jnp.float32, 0.7, 1.3)
    noise_part = jax.random.normal(jax.random.fold_in(key, 27), (SEQ, samples, HID), jnp.float32)
    mixture = amplitude[:, :, None] * chosen + noise_level[None, :, None] * noise_part
    return jnp.clip(mixture, -12.0, 12.0).astype(jnp.bfloat16)


def place_ends(values, key, low, largest):
    extent = values.shape
    spot = [jax.random.randint(jax.random.fold_in(key, axis), (), 0, extent[axis]) for axis in range(len(extent))]
    values = values.at[tuple(spot)].set(low)
    longest = extent.index(max(extent))
    spot[longest] = (spot[longest] + 1) % extent[longest]
    return values.at[tuple(spot)].set(largest)


def block_scale(key, extent, pieces, low, high):
    loudness = 1.0
    for dim, parts in pieces:
        steps = jax.random.uniform(jax.random.fold_in(jax.random.fold_in(key, 6), dim), (parts,), jnp.float32, low / len(pieces), high / len(pieces))
        loudness = loudness * jnp.repeat(jnp.exp(steps), extent[dim] // parts).reshape((-1,) + (1,) * (len(extent) - 1 - dim))
    return loudness


def bell_draw(key, shape, width, most, shards=(), kind=jnp.bfloat16):
    array = jax.random.normal(key, shape, jnp.float32) * width
    if len(shards) > 0:
        array = block_scale(key, shape, shards, -0.22, 0.18) * array
    return jnp.clip(array, min=-most, max=most).astype(kind)


def setup_inputs(seed: int = 0) -> dict:
    key_of = jax.random.split(jax.random.key(seed), 7)
    hidden = draw_hidden(jax.random.fold_in(key_of[6], 71), 0)
    w_proj = bell_draw(key_of[1], (HID, EMB), HID ** -0.5, 0.0625, ((0, 4), (1, 8)))
    slot_prompt = draw_slot_prompt(jax.random.fold_in(key_of[6], 71), 0)
    lengths = place_ends(jax.random.randint(key_of[3], (NS,), 1, SEQ + 1), jax.random.fold_in(key_of[3], 1), 1, SEQ).astype(jnp.int32)
    weights = jnp.clip(jnp.exp(math.log(10.0) - 4.609084 * jax.random.uniform(key_of[4], (NS,), jnp.float32) ** block_scale(key_of[4], (NS,), ((0, 8),), -0.2, 0.2)), 0.099609375, 10.0).astype(jnp.bfloat16)
    owner = jax.random.permutation(key_of[5], N_GEN).astype(jnp.int32)
    return {"hidden": hidden, "w_proj": w_proj, "slot_prompt": slot_prompt, "lengths": lengths, "weights": weights, "owner": owner}


def project_group(hidden, w_proj, group_index):
    part_rows = HID // N_SPLIT
    block = lax.dynamic_slice_in_dim(hidden, group_index * SLOTS, SLOTS, 1)
    summed = jnp.zeros((SEQ, SLOTS, EMB), jnp.float32)
    for feature_part in range(N_SPLIT):
        rows_part = block[:, :, feature_part * part_rows:(feature_part + 1) * part_rows].astype(jnp.float32)
        weight_part = w_proj[feature_part * part_rows:(feature_part + 1) * part_rows].astype(jnp.float32)
        partial_term = jnp.einsum('psh,he->pse', rows_part, weight_part)
        rounded = lax.optimization_barrier(partial_term.astype(jnp.bfloat16))
        summed = summed + rounded.astype(jnp.float32)
    scale = lax.rsqrt(lax.optimization_barrier(jnp.mean(summed * summed, axis=-1, keepdims=True)) + 1e-06) / math.sqrt(EMB)
    return (summed * scale).astype(jnp.bfloat16)

def prompt_utility(embedded, slot_prompt, lengths, weights, prompt):
    member = (slot_prompt == prompt).astype(jnp.int32)
    running = jnp.cumsum(member)
    targets = jnp.arange(MAXS, dtype=jnp.int32)
    position = lax.optimization_barrier(jnp.sum((running[None, :] <= targets[:, None]).astype(jnp.int32), axis=1))
    position = jnp.minimum(position, SLOTS * N_GEN - 1).astype(jnp.int32)
    filled = targets < running[-1]
    member_len = jnp.where(filled, jnp.take(lengths, position), 0).astype(jnp.int32)
    member_weight = jnp.where(filled, jnp.take(weights, position).astype(jnp.float32), jnp.float32(0.0))
    chosen = jnp.take(embedded, position, axis=1)
    flat = chosen.reshape(SEQ * MAXS, EMB)
    sim = jnp.dot(flat, flat.T, preferred_element_type=jnp.float32).reshape(SEQ, MAXS, SEQ, MAXS)
    steps_pos = jnp.arange(SEQ, dtype=jnp.int32)
    col_ok = steps_pos[:, None] < member_len[None, :]
    sim = jnp.where(col_ok[None, None, :, :], sim, jnp.float32(-2.0))
    best = lax.optimization_barrier(jnp.max(sim, axis=2))
    row_ok = steps_pos[:, None] < member_len[None, :]
    summed = lax.optimization_barrier(jnp.sum(jnp.where(row_ok[:, :, None], best, jnp.float32(0.0)), axis=0))
    recall = summed / jnp.maximum(member_len, 1).astype(jnp.float32)[:, None]
    score = 0.5 * (recall + recall.T)
    util = lax.optimization_barrier(jnp.sum(score * member_weight[None, :], axis=1)) / jnp.sum(member_weight)
    return jnp.where(filled, util, jnp.float32(0.0))

def reference(hidden, w_proj, slot_prompt, lengths, weights, owner):
    groups = lax.map(lambda group_index: project_group(hidden, w_proj, group_index), jnp.arange(N_GEN, dtype=jnp.int32))
    embedded = jnp.transpose(groups, (1, 0, 2, 3)).reshape(SEQ, N_GEN * SLOTS, EMB)
    per_prompt = lax.map(lambda prompt: prompt_utility(embedded, slot_prompt, lengths, weights, prompt), jnp.arange(N_GEN, dtype=jnp.int32))
    table = jnp.zeros((N_GEN, MAXS), jnp.float32)
    return table.at[owner].set(per_prompt)
```

```python
import functools
import math

import jax
import jax.numpy as jnp
from jax import lax
from jax.experimental import pallas as pl
from jax.experimental.pallas import tpu as pltpu
from jax.sharding import PartitionSpec as P

MAXS = 64
PAIR = 2
MESH = pl.DeviceIdType.MESH


def greet(n_gen, n_split):
    g = lax.axis_index("gen")
    s = lax.axis_index("split")
    barrier = pltpu.get_barrier_semaphore()
    for i in range(1, n_gen):
        pl.semaphore_signal(
            barrier, inc=1, device_id={"gen": lax.rem(g + i, n_gen)}, device_id_type=MESH
        )
    for i in range(1, n_split):
        pl.semaphore_signal(
            barrier, inc=1, device_id={"split": lax.rem(s + i, n_split)}, device_id_type=MESH
        )
    pl.semaphore_wait(barrier, n_gen + n_split - 2)


def project_kernel(
    n_gen, n_split, h_ref, w_ref, meta_ref, unit_ref, metas_ref,
    h_held, w_held, term, inbox, h_sem, up_sem, down_sem, side_sem, line_sem, cross_sem,
    out_sem, in_sem, meta_send, meta_recv,
):
    g = lax.axis_index("gen")
    s = lax.axis_index("split")
    n_line = n_gen // PAIR
    z, x = g // PAIR, lax.rem(g, PAIR)
    width = w_ref.shape[1]
    rows = h_held.shape[0] // n_split
    load = pltpu.make_async_copy(h_ref, h_held, h_sem)
    load.start()
    greet(n_gen, n_split)

    def shard(line, side):
        return w_held.at[line, :, pl.ds(pl.multiple_of(side * width, width), width)]

    def move(source, line, line_to, side_to, send_sem, recv_sem):
        return pltpu.make_async_remote_copy(
            src_ref=source, dst_ref=shard(line, x), send_sem=send_sem, recv_sem=recv_sem,
            device_id={"gen": line_to * PAIR + side_to}, device_id_type=MESH,
        )

    def up(source, line):
        return move(source, line, z + 1, x, up_sem.at[line], line_sem.at[line])

    def down(source, line):
        return move(source, line, z - 1, x, down_sem.at[line], line_sem.at[line])

    def side(source, line):
        return move(source, line, z, 1 - x, side_sem.at[line], cross_sem.at[line])

    def meta_copy(i):
        peer = lax.rem(g + i, n_gen)
        return pltpu.make_async_remote_copy(
            src_ref=meta_ref, dst_ref=metas_ref.at[g], send_sem=meta_send.at[peer],
            recv_sem=meta_recv.at[g], device_id={"gen": peer}, device_id_type=MESH,
        )

    def landed(ref, sem):
        pltpu.make_async_copy(ref, ref, sem).wait()

    side(w_ref, z).start()

    @pl.when(z < n_line - 1)
    def _():
        up(w_ref, z).start()

    @pl.when(z > 0)
    def _():
        down(w_ref, z).start()

    for i in range(1, n_gen):
        meta_copy(i).start()
    metas_ref[g] = meta_ref[...]
    w_held[z, :, pl.ds(pl.multiple_of(x * width, width), width)] = w_ref[...]
    load.wait()

    def term_copy(line, peer):
        return pltpu.make_async_remote_copy(
            src_ref=term.at[line, peer], dst_ref=inbox.at[line, s], send_sem=out_sem.at[line, peer],
            recv_sem=in_sem.at[line, s], device_id={"split": peer}, device_id_type=MESH,
        )

    def product(line, part):
        start = pl.multiple_of(part * rows, rows)
        return jnp.dot(
            h_held[pl.ds(start, rows), :], w_held[line], preferred_element_type=jnp.float32
        ).astype(jnp.bfloat16)

    def group(line):
        landed(shard(line, 1 - x), cross_sem.at[line])

        def step(i, carry):
            peer = lax.rem(s + i, n_split)
            term[line, peer] = product(line, peer)
            term_copy(line, peer).start()
            return carry

        lax.fori_loop(1, n_split, step, 0)
        inbox[line, s] = product(line, s)

    def group_at(distance):
        if distance == 0:
            group(z)
            return

        @pl.when(z - distance >= 0)
        def _():
            group(z - distance)

        @pl.when(z + distance < n_line)
        def _():
            group(z + distance)

    for distance in range(1, n_line):

        @pl.when(z - distance >= 0)
        def _():
            line = z - distance
            landed(shard(line, x), line_sem.at[line])

            @pl.when(z < n_line - 1)
            def _():
                up(shard(line, x), line).start()

            side(shard(line, x), line).start()

        @pl.when(z + distance < n_line)
        def _():
            line = z + distance
            landed(shard(line, x), line_sem.at[line])

            @pl.when(z > 0)
            def _():
                down(shard(line, x), line).start()

            side(shard(line, x), line).start()

        group_at(distance - 1)
    group_at(n_line - 1)

    for line in range(n_line):
        for i in range(1, n_split):
            peer = lax.rem(s + i, n_split)
            landed(inbox.at[line, peer], in_sem.at[line, peer])
    chunk = 64
    full = unit_ref.shape[1]
    wide = PAIR * width

    @pl.loop(0, rows // chunk)
    def _(c):
        here = pl.ds(pl.multiple_of(c * chunk, chunk), chunk)
        squares = jnp.zeros((chunk, 1), jnp.float32)
        sums = []
        for line in range(n_line):
            total = inbox[line, 0, here, :].astype(jnp.float32)
            for part in range(1, n_split):
                total = total + inbox[line, part, here, :].astype(jnp.float32)
            squares = squares + jnp.sum(total * total, axis=1, keepdims=True)
            sums.append(total)
        scale = lax.rsqrt(squares / full + 1e-06) / math.sqrt(full)
        for line in range(n_line):
            unit_ref[here, line * wide : (line + 1) * wide] = (sums[line] * scale).astype(jnp.bfloat16)

    for i in range(1, n_gen):
        peer = lax.rem(g + i, n_gen)
        landed(metas_ref.at[peer], meta_recv.at[peer])
        meta_copy(i).wait_send()
    for line in range(n_line):
        side(shard(line, x), line).wait_send()

        @pl.when((z < n_line - 1) & (line <= z))
        def _():
            up(shard(line, x), line).wait_send()

        @pl.when((z > 0) & (line >= z))
        def _():
            down(shard(line, x), line).wait_send()

        for i in range(1, n_split):
            term_copy(line, lax.rem(s + i, n_split)).wait_send()


def project(hidden, w_proj, meta, n_gen, n_split):
    h = hidden.reshape(hidden.shape[0] * hidden.shape[1], hidden.shape[2])
    depth, width = w_proj.shape
    n_line = n_gen // PAIR
    rows = h.shape[0] // n_split
    wide = PAIR * width
    dma = pltpu.SemaphoreType.DMA
    vmem = pl.BlockSpec(memory_space=pltpu.VMEM)
    return pl.pallas_call(
        functools.partial(project_kernel, n_gen, n_split),
        out_shape=(
            jax.ShapeDtypeStruct((rows, n_gen * width), jnp.bfloat16),
            jax.ShapeDtypeStruct((n_gen,) + meta.shape, jnp.float32),
        ),
        in_specs=[pl.BlockSpec(memory_space=pl.ANY), vmem, vmem],
        out_specs=(vmem, vmem),
        scratch_shapes=[
            pltpu.VMEM(h.shape, jnp.bfloat16),
            pltpu.VMEM((n_line, depth, wide), jnp.bfloat16),
            pltpu.VMEM((n_line, n_split, rows, wide), jnp.bfloat16),
            pltpu.VMEM((n_line, n_split, rows, wide), jnp.bfloat16),
            dma, dma((n_line,)), dma((n_line,)), dma((n_line,)), dma((n_line,)), dma((n_line,)),
            dma((n_line, n_split)), dma((n_line, n_split)), dma((n_gen,)), dma((n_gen,)),
        ],
        compiler_params=pltpu.CompilerParams(
            collective_id=0, has_side_effects=True, vmem_limit_bytes=40 * 1024 * 1024
        ),
        cost_estimate=pl.CostEstimate(
            flops=2 * h.shape[0] * depth * n_gen * width, bytes_accessed=h.size * 2, transcendentals=0
        ),
    )(h, w_proj, meta)


def column_best(row_flat, gathered, member_len):
    amount = gathered.shape[0]
    slots_here = gathered.shape[1]
    col_flat = gathered.reshape(amount * slots_here, gathered.shape[2])
    scores = lax.dot_general(
        row_flat, col_flat, (((1,), (1,)), ((), ())), preferred_element_type=jnp.float32
    )
    scores = scores.reshape(row_flat.shape[0] // slots_here, slots_here, amount, slots_here)
    positions = jnp.arange(amount, dtype=jnp.int32)
    col_ok = positions[:, None] < member_len[None, :]
    scores = jnp.where(col_ok[None, None, :, :], scores, jnp.float32(-2.0))
    return jnp.max(scores, axis=2)


def unit_plain(hidden, w_proj):
    w_block = lax.all_gather(w_proj, "gen", axis=1, tiled=True)
    emb_width = w_block.shape[1]
    projected = lax.psum_scatter(
        jnp.einsum("psh,he->pse", hidden, w_block, preferred_element_type=jnp.float32).astype(
            jnp.bfloat16
        ),
        "split",
        scatter_dimension=0,
        tiled=True,
    ).astype(jnp.float32)
    scale = lax.rsqrt(jnp.mean(projected * projected, axis=-1, keepdims=True) + 1e-06) / math.sqrt(
        emb_width
    )
    unit = (projected * scale).astype(jnp.bfloat16)
    return unit


def body(hidden, w_proj, slot_prompt, lengths, weights, owner):
    n_gen = lax.axis_size("gen")
    n_split = lax.axis_size("split")
    seq_part = hidden.shape[0] // n_split
    slots = hidden.shape[1]
    emb_width = w_proj.shape[1] * n_gen
    if w_proj.shape[1] % 128 == 0 and n_gen % PAIR == 0:
        meta = jnp.zeros((8, 128), jnp.float32)
        unit, metas = project(hidden, w_proj, meta, n_gen, n_split)
        unit = unit.reshape(seq_part, slots, emb_width)
    else:
        unit = unit_plain(hidden, w_proj)
    owner_cap = (MAXS + n_gen - 1) // n_gen
    buffer_slots = n_gen * owner_cap
    owner_hit = slot_prompt[:, None] == jnp.arange(n_gen, dtype=jnp.int32)[None, :]
    dest_owner = jnp.sum(jnp.where(owner_hit, owner[None, :], 0), axis=1)
    local_index = jnp.arange(slots, dtype=jnp.int32)
    same_prompt = slot_prompt[:, None] == slot_prompt[None, :]
    earlier = local_index[:, None] > local_index[None, :]
    rank = jnp.sum((same_prompt & earlier).astype(jnp.int32), axis=1)
    destination = dest_owner * owner_cap + rank
    matches = destination[None, :] == jnp.arange(buffer_slots, dtype=jnp.int32)[:, None]
    occupied = jnp.sum(matches.astype(jnp.int32), axis=1) > 0
    source_slot = jnp.sum(jnp.where(matches, local_index[None, :], 0), axis=1)
    send_unit = jnp.take(unit, source_slot, axis=1)
    send_len = jnp.where(occupied, jnp.take(lengths, source_slot), 0).astype(jnp.bfloat16)
    send_weight = jnp.where(occupied, jnp.take(weights, source_slot), jnp.zeros((), jnp.bfloat16))
    send_meta = jnp.stack([send_len, send_weight], axis=0)
    arrived, arrived_meta = (
        lax.all_to_all(send_unit, "gen", split_axis=1, concat_axis=1, tiled=True),
        lax.all_to_all(send_meta, "gen", split_axis=1, concat_axis=1, tiled=True),
    )
    arrived_len = arrived_meta[0].astype(jnp.int32)
    arrived_weight = arrived_meta[1].astype(jnp.float32)
    running = jnp.cumsum((arrived_len > 0).astype(jnp.int32))
    targets = jnp.arange(MAXS, dtype=jnp.int32)
    position = jnp.sum((running[None, :] <= targets[:, None]).astype(jnp.int32), axis=1)
    position = jnp.minimum(position, buffer_slots - 1)
    filled = targets < running[-1]
    member_len = jnp.where(filled, jnp.take(arrived_len, position), 0)
    member_weight = jnp.where(filled, jnp.take(arrived_weight, position), jnp.float32(0.0))
    mine = jnp.take(arrived, position, axis=1)
    row_flat = mine.reshape(seq_part * MAXS, emb_width)
    every = lax.all_gather(arrived, "split", axis=0, tiled=True)
    columns = jnp.take(every, position, axis=1)
    best = column_best(row_flat, columns, member_len)
    my_positions = lax.axis_index("split") * seq_part + jnp.arange(seq_part, dtype=jnp.int32)
    row_ok = my_positions[:, None] < member_len[None, :]
    partial_sums = jnp.sum(jnp.where(row_ok[:, :, None], best, jnp.float32(0.0)), axis=0)
    summed = lax.psum(partial_sums, "split")
    recall = summed / jnp.maximum(member_len, 1).astype(jnp.float32)[:, None]
    score = 0.5 * (recall + recall.T)
    util = jnp.sum(score * member_weight[None, :], axis=1) / jnp.sum(member_weight)
    util = jnp.where(filled, util, jnp.float32(0.0))
    return util[None, :]


def solution(mesh):
    placed = (P(None, "gen", "split"), P("split", "gen"), P("gen"), P("gen"), P("gen"), P())
    return jax.shard_map(
        body, mesh=mesh, in_specs=placed, out_specs=P("gen", None), check_vma=False
    )
```

```python
import functools
import math

import jax
import jax.numpy as jnp
from jax import lax
from jax.experimental import pallas as pl
from jax.experimental.pallas import tpu as pltpu
from jax.sharding import PartitionSpec as P

MAXS = 64
PAIR = 2
MESH = pl.DeviceIdType.MESH


def greet(n_gen, n_split):
    g = lax.axis_index("gen")
    s = lax.axis_index("split")
    barrier = pltpu.get_barrier_semaphore()
    for i in range(1, n_gen):
        pl.semaphore_signal(
            barrier, inc=1, device_id={"gen": lax.rem(g + i, n_gen)}, device_id_type=MESH
        )
    for i in range(1, n_split):
        pl.semaphore_signal(
            barrier, inc=1, device_id={"split": lax.rem(s + i, n_split)}, device_id_type=MESH
        )
    pl.semaphore_wait(barrier, n_gen + n_split - 2)


def project_kernel(
    n_gen, n_split, h_ref, w_ref, meta_ref, unit_ref, metas_ref,
    h_held, w_held, term, inbox, h_sem, up_sem, down_sem, side_sem, line_sem, cross_sem,
    out_sem, in_sem, meta_send, meta_recv,
):
    g = lax.axis_index("gen")
    s = lax.axis_index("split")
    n_line = n_gen // PAIR
    z, x = g // PAIR, lax.rem(g, PAIR)
    width = w_ref.shape[1]
    rows = h_held.shape[0] // n_split
    load = pltpu.make_async_copy(h_ref, h_held, h_sem)
    load.start()
    greet(n_gen, n_split)

    def shard(line, side):
        return w_held.at[line, :, pl.ds(pl.multiple_of(side * width, width), width)]

    def move(source, line, line_to, side_to, send_sem, recv_sem):
        return pltpu.make_async_remote_copy(
            src_ref=source, dst_ref=shard(line, x), send_sem=send_sem, recv_sem=recv_sem,
            device_id={"gen": line_to * PAIR + side_to}, device_id_type=MESH,
        )

    def up(source, line):
        return move(source, line, z + 1, x, up_sem.at[line], line_sem.at[line])

    def down(source, line):
        return move(source, line, z - 1, x, down_sem.at[line], line_sem.at[line])

    def side(source, line):
        return move(source, line, z, 1 - x, side_sem.at[line], cross_sem.at[line])

    def meta_copy(i):
        peer = lax.rem(g + i, n_gen)
        return pltpu.make_async_remote_copy(
            src_ref=meta_ref, dst_ref=metas_ref.at[g], send_sem=meta_send.at[peer],
            recv_sem=meta_recv.at[g], device_id={"gen": peer}, device_id_type=MESH,
        )

    def landed(ref, sem):
        pltpu.make_async_copy(ref, ref, sem).wait()

    side(w_ref, z).start()

    @pl.when(z < n_line - 1)
    def _():
        up(w_ref, z).start()

    @pl.when(z > 0)
    def _():
        down(w_ref, z).start()

    for i in range(1, n_gen):
        meta_copy(i).start()
    metas_ref[g] = meta_ref[...]
    w_held[z, :, pl.ds(pl.multiple_of(x * width, width), width)] = w_ref[...]
    load.wait()

    def term_copy(line, peer):
        return pltpu.make_async_remote_copy(
            src_ref=term.at[line, peer], dst_ref=inbox.at[line, s], send_sem=out_sem.at[line, peer],
            recv_sem=in_sem.at[line, s], device_id={"split": peer}, device_id_type=MESH,
        )

    def product(line, part):
        start = pl.multiple_of(part * rows, rows)
        return jnp.dot(
            h_held[pl.ds(start, rows), :], w_held[line], preferred_element_type=jnp.float32
        ).astype(jnp.bfloat16)

    def group(line):
        landed(shard(line, 1 - x), cross_sem.at[line])

        def step(i, carry):
            peer = lax.rem(s + i, n_split)
            term[line, peer] = product(line, peer)
            term_copy(line, peer).start()
            return carry

        lax.fori_loop(1, n_split, step, 0)
        inbox[line, s] = product(line, s)

    def group_at(distance):
        if distance == 0:
            group(z)
            return

        @pl.when(z - distance >= 0)
        def _():
            group(z - distance)

        @pl.when(z + distance < n_line)
        def _():
            group(z + distance)

    for distance in range(1, n_line):

        @pl.when(z - distance >= 0)
        def _():
            line = z - distance
            landed(shard(line, x), line_sem.at[line])

            @pl.when(z < n_line - 1)
            def _():
                up(shard(line, x), line).start()

            side(shard(line, x), line).start()

        @pl.when(z + distance < n_line)
        def _():
            line = z + distance
            landed(shard(line, x), line_sem.at[line])

            @pl.when(z > 0)
            def _():
                down(shard(line, x), line).start()

            side(shard(line, x), line).start()

        group_at(distance - 1)
    group_at(n_line - 1)

    for line in range(n_line):
        for i in range(1, n_split):
            peer = lax.rem(s + i, n_split)
            landed(inbox.at[line, peer], in_sem.at[line, peer])
    chunk = 64
    full = unit_ref.shape[1]
    wide = PAIR * width

    @pl.loop(0, rows // chunk)
    def _(c):
        here = pl.ds(pl.multiple_of(c * chunk, chunk), chunk)
        squares = jnp.zeros((chunk, 1), jnp.float32)
        sums = []
        for line in range(n_line):
            total = inbox[line, 0, here, :].astype(jnp.float32)
            for part in range(1, n_split):
                total = total + inbox[line, part, here, :].astype(jnp.float32)
            squares = squares + jnp.sum(total * total, axis=1, keepdims=True)
            sums.append(total)
        scale = lax.rsqrt(squares / full + 1e-06) / math.sqrt(full)
        for line in range(n_line):
            unit_ref[here, line * wide : (line + 1) * wide] = (sums[line] * scale).astype(jnp.bfloat16)

    for i in range(1, n_gen):
        peer = lax.rem(g + i, n_gen)
        landed(metas_ref.at[peer], meta_recv.at[peer])
        meta_copy(i).wait_send()
    for line in range(n_line):
        side(shard(line, x), line).wait_send()

        @pl.when((z < n_line - 1) & (line <= z))
        def _():
            up(shard(line, x), line).wait_send()

        @pl.when((z > 0) & (line >= z))
        def _():
            down(shard(line, x), line).wait_send()

        for i in range(1, n_split):
            term_copy(line, lax.rem(s + i, n_split)).wait_send()


def project(hidden, w_proj, meta, n_gen, n_split):
    h = hidden.reshape(hidden.shape[0] * hidden.shape[1], hidden.shape[2])
    depth, width = w_proj.shape
    n_line = n_gen // PAIR
    rows = h.shape[0] // n_split
    wide = PAIR * width
    dma = pltpu.SemaphoreType.DMA
    vmem = pl.BlockSpec(memory_space=pltpu.VMEM)
    return pl.pallas_call(
        functools.partial(project_kernel, n_gen, n_split),
        out_shape=(
            jax.ShapeDtypeStruct((rows, n_gen * width), jnp.bfloat16),
            jax.ShapeDtypeStruct((n_gen,) + meta.shape, jnp.float32),
        ),
        in_specs=[pl.BlockSpec(memory_space=pl.ANY), vmem, vmem],
        out_specs=(vmem, vmem),
        scratch_shapes=[
            pltpu.VMEM(h.shape, jnp.bfloat16),
            pltpu.VMEM((n_line, depth, wide), jnp.bfloat16),
            pltpu.VMEM((n_line, n_split, rows, wide), jnp.bfloat16),
            pltpu.VMEM((n_line, n_split, rows, wide), jnp.bfloat16),
            dma, dma((n_line,)), dma((n_line,)), dma((n_line,)), dma((n_line,)), dma((n_line,)),
            dma((n_line, n_split)), dma((n_line, n_split)), dma((n_gen,)), dma((n_gen,)),
        ],
        compiler_params=pltpu.CompilerParams(
            collective_id=0, has_side_effects=True, vmem_limit_bytes=40 * 1024 * 1024
        ),
        cost_estimate=pl.CostEstimate(
            flops=2 * h.shape[0] * depth * n_gen * width, bytes_accessed=h.size * 2, transcendentals=0
        ),
    )(h, w_proj, meta)


def match_kernel(
    n_gen, n_split, cap, unit_ref, sel_ref, len_ref, mask_ref, out_ref, staging, held, sums,
    send_sem, recv_sem, far_send, far_recv, near_send, near_recv, sum_send, sum_recv,
):
    g = lax.axis_index("gen")
    s = lax.axis_index("split")
    far = lax.rem(s + 2, n_split)
    near = s + 1 - 2 * lax.rem(s, 2)
    near_far = lax.rem(near + 2, n_split)
    block = staging.shape[1]
    positions = block // cap
    greet(n_gen, n_split)

    def landed(ref, sem):
        pltpu.make_async_copy(ref, ref, sem).wait()

    def deliver(i):
        peer = lax.rem(g + i, n_gen)
        return pltpu.make_async_remote_copy(
            src_ref=staging.at[peer], dst_ref=held.at[s, g], send_sem=send_sem.at[peer],
            recv_sem=recv_sem.at[g], device_id={"gen": peer}, device_id_type=MESH,
        )

    def share(part, source, to, out_sem, in_sem):
        return pltpu.make_async_remote_copy(
            src_ref=held.at[part, source], dst_ref=held.at[part, source], send_sem=out_sem,
            recv_sem=in_sem, device_id={"split": to}, device_id_type=MESH,
        )

    def to_far(source):
        return share(s, source, far, far_send.at[source], far_recv.at[source])

    def to_near(source):
        return share(s, source, near, near_send.at[0, source], near_recv.at[0, source])

    def relay(source):
        return share(far, source, near, near_send.at[1, source], near_recv.at[1, source])

    def stage(peer):
        return jnp.dot(
            sel_ref[peer], unit_ref[...], preferred_element_type=jnp.float32
        ).astype(jnp.bfloat16)

    for i in range(1, n_gen):
        peer = lax.rem(g + i, n_gen)
        staging[peer] = stage(peer)
        deliver(i).start()
    held[s, g] = stage(g)
    to_far(g).start()
    to_near(g).start()
    for i in range(1, n_gen + 1):
        if i < n_gen:
            source = lax.rem(g + n_gen - i, n_gen)
            landed(held.at[s, source], recv_sem.at[source])
            to_far(source).start()
            to_near(source).start()
        before = lax.rem(g + n_gen - (i - 1), n_gen)
        landed(held.at[far, before], far_recv.at[before])
        relay(before).start()

    full = held.shape[3]
    rows = held[s].reshape(n_gen * block, full)
    lens = len_ref[...].reshape(n_gen, 1, cap, 1)

    def part_best(part):
        sim = lax.dot_general(
            held[part].reshape(n_gen * block, full), rows, (((1,), (1,)), ((), ())),
            preferred_element_type=jnp.float32,
        ).reshape(n_gen, positions, cap, n_gen * block)
        at = part * positions + lax.broadcasted_iota(jnp.int32, (n_gen, positions, cap, 1), 1)
        return jnp.max(jnp.where(at < lens, sim, jnp.float32(-2.0)), axis=1)

    best = jnp.maximum(part_best(s), part_best(far))
    for source in range(n_gen):
        landed(held.at[near, source], near_recv.at[0, source])
    best = jnp.maximum(best, part_best(near))
    for source in range(n_gen):
        landed(held.at[near_far, source], near_recv.at[1, source])
    best = jnp.maximum(best, part_best(near_far))
    sums[s] = jnp.dot(
        best.reshape(n_gen * cap, n_gen * block), mask_ref[...],
        preferred_element_type=jnp.float32, precision=lax.Precision.HIGHEST,
    )

    def sum_copy(i):
        peer = lax.rem(s + i, n_split)
        return pltpu.make_async_remote_copy(
            src_ref=sums.at[s], dst_ref=sums.at[s], send_sem=sum_send.at[peer],
            recv_sem=sum_recv.at[s], device_id={"split": peer}, device_id_type=MESH,
        )

    for i in range(1, n_split):
        sum_copy(i).start()
    for i in range(1, n_split):
        peer = lax.rem(s + i, n_split)
        landed(sums.at[peer], sum_recv.at[peer])
    total = sums[0]
    for part in range(1, n_split):
        total = total + sums[part]
    out_ref[...] = total
    for i in range(1, n_split):
        sum_copy(i).wait_send()
    for i in range(1, n_gen):
        deliver(i).wait_send()
    for source in range(n_gen):
        to_far(source).wait_send()
        to_near(source).wait_send()
        relay(source).wait_send()


def match(unit, sel, member_len, mask, n_gen, n_split, cap):
    block, full = sel.shape[1], unit.shape[1]
    dma = pltpu.SemaphoreType.DMA
    vmem = pl.BlockSpec(memory_space=pltpu.VMEM)
    return pl.pallas_call(
        functools.partial(match_kernel, n_gen, n_split, cap),
        out_shape=jax.ShapeDtypeStruct((n_gen * cap, 128), jnp.float32),
        in_specs=[vmem] * 4,
        out_specs=vmem,
        scratch_shapes=[
            pltpu.VMEM((n_gen, block, full), jnp.bfloat16),
            pltpu.VMEM((n_split, n_gen, block, full), jnp.bfloat16),
            pltpu.VMEM((n_split, n_gen * cap, 128), jnp.float32),
            dma((n_gen,)), dma((n_gen,)), dma((n_gen,)), dma((n_gen,)), dma((2, n_gen)),
            dma((2, n_gen)), dma((n_split,)), dma((n_split,)),
        ],
        compiler_params=pltpu.CompilerParams(
            collective_id=1, has_side_effects=True, vmem_limit_bytes=40 * 1024 * 1024
        ),
    )(unit, sel, member_len, mask)


def fused(hidden, w_proj, slot_prompt, lengths, weights, owner):
    n_gen = lax.axis_size("gen")
    n_split = lax.axis_size("split")
    slots = hidden.shape[1]
    positions = hidden.shape[0] // n_split
    cap = MAXS // n_gen
    f32 = jnp.float32
    meta = jnp.stack([slot_prompt.astype(f32), lengths.astype(f32), weights.astype(f32)])
    meta = jnp.pad(meta, ((0, 5), (0, 128 - slots)))
    unit, metas = project(hidden, w_proj, meta, n_gen, n_split)
    ids = jnp.arange(n_gen, dtype=jnp.int32)
    dest = jnp.sum(jnp.where(slot_prompt[:, None] == ids[None, :], owner[None, :], 0), axis=1)
    local = jnp.arange(slots, dtype=jnp.int32)
    same = (slot_prompt[:, None] == slot_prompt[None, :]) & (local[:, None] > local[None, :])
    key = dest * cap + jnp.sum(same.astype(jnp.int32), axis=1)
    place = jnp.arange(positions, dtype=jnp.int32)
    lane = jnp.arange(cap, dtype=jnp.int32)
    sel = (key[None, None, None, None, :] == (ids[:, None] * cap + lane)[:, None, :, None, None]) & (
        place[None, :, None, None, None] == place[None, None, None, :, None]
    )
    sel = sel.astype(jnp.bfloat16).reshape(n_gen, positions * cap, positions * slots)
    mine = jnp.sum(jnp.where(owner == lax.axis_index("gen"), ids, 0))
    hit = metas[:, 0, :slots] == mine.astype(f32)
    rank = jnp.sum((hit[:, None, :] & (local[:, None] > local[None, :])[None]).astype(jnp.int32), axis=2)
    pick = hit[:, None, :] & (rank[:, None, :] == lane[None, :, None])
    member_len = jnp.sum(jnp.where(pick, metas[:, None, 1, :slots], 0.0), axis=2).reshape(MAXS).astype(jnp.int32)
    member_weight = jnp.sum(jnp.where(pick, metas[:, None, 2, :slots], 0.0), axis=2).reshape(MAXS)
    member = (ids[:, None, None] * cap + lane + 0 * place[:, None]).reshape(-1)
    time = lax.axis_index("split") * positions + (place[:, None] + 0 * ids[:, None, None] + 0 * lane).reshape(-1)
    column = jnp.arange(128, dtype=jnp.int32)
    wide_len = jnp.pad(member_len, (0, 128 - MAXS))
    mask = ((member[:, None] == column[None, :]) & (time[:, None] < wide_len[None, :])).astype(f32)
    summed = match(unit, sel, member_len[:, None], mask, n_gen, n_split, cap)[:, :MAXS]
    recall = summed / jnp.maximum(member_len, 1).astype(f32)[None, :]
    score = 0.5 * (recall + recall.T)
    util = jnp.sum(score * member_weight[None, :], axis=1) / jnp.sum(member_weight)
    live = member_len > 0
    order = jnp.arange(MAXS, dtype=jnp.int32)
    spot = jnp.sum((live[None, :] & (order[None, :] < order[:, None])).astype(jnp.int32), axis=1)
    chosen = live[None, :] & (spot[None, :] == order[:, None])
    return jnp.sum(jnp.where(chosen, util[None, :], 0.0), axis=1)[None, :]


def column_best(row_flat, gathered, member_len):
    amount = gathered.shape[0]
    slots_here = gathered.shape[1]
    col_flat = gathered.reshape(amount * slots_here, gathered.shape[2])
    scores = lax.dot_general(
        row_flat, col_flat, (((1,), (1,)), ((), ())), preferred_element_type=jnp.float32
    )
    scores = scores.reshape(row_flat.shape[0] // slots_here, slots_here, amount, slots_here)
    positions = jnp.arange(amount, dtype=jnp.int32)
    col_ok = positions[:, None] < member_len[None, :]
    scores = jnp.where(col_ok[None, None, :, :], scores, jnp.float32(-2.0))
    return jnp.max(scores, axis=2)


def unit_plain(hidden, w_proj):
    w_block = lax.all_gather(w_proj, "gen", axis=1, tiled=True)
    emb_width = w_block.shape[1]
    projected = lax.psum_scatter(
        jnp.einsum("psh,he->pse", hidden, w_block, preferred_element_type=jnp.float32).astype(
            jnp.bfloat16
        ),
        "split",
        scatter_dimension=0,
        tiled=True,
    ).astype(jnp.float32)
    scale = lax.rsqrt(jnp.mean(projected * projected, axis=-1, keepdims=True) + 1e-06) / math.sqrt(
        emb_width
    )
    unit = (projected * scale).astype(jnp.bfloat16)
    return unit


def body(hidden, w_proj, slot_prompt, lengths, weights, owner):
    n_gen = lax.axis_size("gen")
    n_split = lax.axis_size("split")
    seq_part = hidden.shape[0] // n_split
    slots = hidden.shape[1]
    unit = unit_plain(hidden, w_proj)
    emb_width = unit.shape[2]
    owner_cap = (MAXS + n_gen - 1) // n_gen
    buffer_slots = n_gen * owner_cap
    owner_hit = slot_prompt[:, None] == jnp.arange(n_gen, dtype=jnp.int32)[None, :]
    dest_owner = jnp.sum(jnp.where(owner_hit, owner[None, :], 0), axis=1)
    local_index = jnp.arange(slots, dtype=jnp.int32)
    same_prompt = slot_prompt[:, None] == slot_prompt[None, :]
    earlier = local_index[:, None] > local_index[None, :]
    rank = jnp.sum((same_prompt & earlier).astype(jnp.int32), axis=1)
    destination = dest_owner * owner_cap + rank
    matches = destination[None, :] == jnp.arange(buffer_slots, dtype=jnp.int32)[:, None]
    occupied = jnp.sum(matches.astype(jnp.int32), axis=1) > 0
    source_slot = jnp.sum(jnp.where(matches, local_index[None, :], 0), axis=1)
    send_unit = jnp.take(unit, source_slot, axis=1)
    send_len = jnp.where(occupied, jnp.take(lengths, source_slot), 0).astype(jnp.bfloat16)
    send_weight = jnp.where(occupied, jnp.take(weights, source_slot), jnp.zeros((), jnp.bfloat16))
    send_meta = jnp.stack([send_len, send_weight], axis=0)
    arrived, arrived_meta = (
        lax.all_to_all(send_unit, "gen", split_axis=1, concat_axis=1, tiled=True),
        lax.all_to_all(send_meta, "gen", split_axis=1, concat_axis=1, tiled=True),
    )
    arrived_len = arrived_meta[0].astype(jnp.int32)
    arrived_weight = arrived_meta[1].astype(jnp.float32)
    running = jnp.cumsum((arrived_len > 0).astype(jnp.int32))
    targets = jnp.arange(MAXS, dtype=jnp.int32)
    position = jnp.sum((running[None, :] <= targets[:, None]).astype(jnp.int32), axis=1)
    position = jnp.minimum(position, buffer_slots - 1)
    filled = targets < running[-1]
    member_len = jnp.where(filled, jnp.take(arrived_len, position), 0)
    member_weight = jnp.where(filled, jnp.take(arrived_weight, position), jnp.float32(0.0))
    mine = jnp.take(arrived, position, axis=1)
    row_flat = mine.reshape(seq_part * MAXS, emb_width)
    every = lax.all_gather(arrived, "split", axis=0, tiled=True)
    columns = jnp.take(every, position, axis=1)
    best = column_best(row_flat, columns, member_len)
    my_positions = lax.axis_index("split") * seq_part + jnp.arange(seq_part, dtype=jnp.int32)
    row_ok = my_positions[:, None] < member_len[None, :]
    partial_sums = jnp.sum(jnp.where(row_ok[:, :, None], best, jnp.float32(0.0)), axis=0)
    summed = lax.psum(partial_sums, "split")
    recall = summed / jnp.maximum(member_len, 1).astype(jnp.float32)[:, None]
    score = 0.5 * (recall + recall.T)
    util = jnp.sum(score * member_weight[None, :], axis=1) / jnp.sum(member_weight)
    util = jnp.where(filled, util, jnp.float32(0.0))
    return util[None, :]


def solution(mesh):
    n_gen, n_split = mesh.shape["gen"], mesh.shape["split"]
    narrow = n_gen % PAIR == 0 and MAXS % n_gen == 0 and n_gen <= 8 and n_split == 4
    placed = (P(None, "gen", "split"), P("split", "gen"), P("gen"), P("gen"), P("gen"), P())
    return jax.shard_map(
        fused if narrow else body, mesh=mesh, in_specs=placed, out_specs=P("gen", None), check_vma=False
    )
```
